32 devices in a mesh: crops: 2 (over x), rows: 16 (over z, y, core).
Axes of the slice: x: 2, y: 2, z: 4, core: 2. Of those that a mesh axis runs over, the one named last changes fastest.
Arguments:
- features: bfloat16 [64, 128, 2048], P(('crops', 'rows')), parts along dimension 0, may hold values from -6 to 6
- bn_scale: float32 [2048], replicated, may hold values from 0.25 to 1.75
- bn_shift: float32 [2048], replicated, may hold values from -0.6 to 0.6
- atrous_weight: bfloat16 [3, 3, 2048, 256], replicated, may hold values from -0.046875 to 0.046875
- cotangent: bfloat16 [64, 128, 256], P(('crops', 'rows')), parts along dimension 0, may hold values from -0.59765625 to 0.59765625
Outputs:
- branch_out: bfloat16 [64, 128, 256], P(('crops', 'rows')), parts along dimension 0
- feature_grad: bfloat16 [64, 128, 2048], P(('crops', 'rows')), parts along dimension 0
- weight_grad: float32 [6, 3, 2048, 256], P('crops', None, 'rows'), parts along dimension 0
The draws below stay inside these ranges and needn't reach their ends.
There are 2 independent parts, one for each index of `crops`. The reference program is written for one: setup_inputs(seed, part) draws one part's arguments, and reference() takes and returns one part's arrays. A program takes and returns all parts, laid end to end along the dimension named above; an argument that names none is the same for every part. Nothing has to cross between parts.
All inputs are finite; a program needn't handle non-finite values.
Results may differ from the reference program's by a relative error of at most 0.0051.
Values may be sent and summed in bfloat16 or wider, within the bound.
A program may use at most 128 MiB of HBM per device.

```python
import jax
import jax.numpy as jnp
from jax import lax

C = 2048
CO = 256
RATE = 12
W = 128
H = 32


def level_of(stream_key, extent, pieces, least, top_value):
    def one(position, blocks):
        steps = jax.random.uniform(jax.random.fold_in(jax.random.fold_in(stream_key, 6), position), (blocks,), jnp.float32, least / len(pieces), top_value / len(pieces))
        return jnp.repeat(jnp.exp(steps), extent[position] // blocks).reshape((-1,) + (1,) * (len(extent) - position - 1))

    factor_of = one(*pieces[0])
    for cut in pieces[1:]:
        factor_of = factor_of * one(*cut)
    return factor_of


def gaussian(rng, extent, spread, reach, shards=(), held_as=jnp.bfloat16):
    drawn = jax.random.normal(rng, extent, jnp.float32) * spread
    if len(shards) > 0:
        drawn = level_of(rng, extent, shards, -0.22, 0.18) * drawn
    return jnp.clip(drawn, min=-reach, max=reach).astype(held_as)


def setup_inputs(seed: int = 0, part: int = 0) -> dict:
    seeds = jax.random.split(jax.random.key(seed), 6)
    own_keys = jax.random.split(jax.random.fold_in(seeds[5], part), 6)
    return {
        "features": gaussian(own_keys[0], (H, W, C), 1.0, 6.0, ((0, 16),)),
        "bn_scale": jnp.clip(1.0 + 0.15 * jax.random.normal(seeds[1], (C,), jnp.float32), 0.25, 1.75),
        "bn_shift": jnp.clip(jax.random.uniform(seeds[2], (C,), jnp.float32, -0.6, 0.6), -0.6, 0.6),
        "atrous_weight": gaussian(seeds[3], (3, 3, C, CO), (9 * C) ** -0.5, 0.046875),
        "cotangent": gaussian(own_keys[4], (H, W, CO), 0.1, 0.59765625, ((0, 16),)),
    }


def reference(features, bn_scale, bn_shift, atrous_weight, cotangent):
    height, width, chans = features.shape
    outs = cotangent.shape[2]
    pre_act = features.astype(jnp.float32) * bn_scale + bn_shift
    activated = jnp.maximum(pre_act, 0.0).astype(jnp.bfloat16)
    padded = jnp.pad(activated, ((RATE, RATE), (RATE, RATE), (0, 0)))
    grad_pad = jnp.pad(cotangent, ((RATE, RATE), (RATE, RATE), (0, 0)))
    flat_cot = cotangent.reshape(height * width, outs)
    branch = jnp.zeros((height * width, outs), jnp.float32)
    act_grad = jnp.zeros((height * width, chans), jnp.float32)
    kernel_rows = []
    for row_tap in range(3):
        kernel_cols = []
        for col_tap in range(3):
            window = padded[RATE * row_tap:RATE * row_tap + height, RATE * col_tap:RATE * col_tap + width]
            window = window.reshape(height * width, chans)
            tap_weight = atrous_weight[row_tap, col_tap]
            branch = branch + jnp.dot(window, tap_weight, preferred_element_type=jnp.float32)
            kernel_cols.append(jnp.dot(window.T, flat_cot, preferred_element_type=jnp.float32))
            back_window = grad_pad[RATE * (2 - row_tap):RATE * (2 - row_tap) + height, RATE * (2 - col_tap):RATE * (2 - col_tap) + width]
            back_window = back_window.reshape(height * width, outs)
            act_grad = act_grad + jnp.dot(back_window, tap_weight.T, preferred_element_type=jnp.float32)
        kernel_rows.append(jnp.stack(kernel_cols))
    weight_grad = jnp.stack(kernel_rows)
    branch_out = branch.reshape(height, width, outs).astype(jnp.bfloat16)
    rounded = lax.optimization_barrier(act_grad.astype(jnp.bfloat16)).astype(jnp.float32)
    rounded = rounded.reshape(height, width, chans)
    feature_grad = (bn_scale * jnp.where(pre_act > 0, rounded, 0.0)).astype(jnp.bfloat16)
    return branch_out, feature_grad, weight_grad
```

```python
import functools

import jax
import jax.numpy as jnp
from jax import lax
from jax.experimental import pallas as pl
from jax.experimental.pallas import tpu as pltpu
from jax.sharding import PartitionSpec as P

RATE = 12
LANES = 128
BF16 = jnp.bfloat16
F32 = jnp.float32


def col_shift(x, tap):
    if tap == 1:
        return x
    rows, width, _ = x.shape
    column = lax.broadcasted_iota(jnp.int32, x.shape[1:], 0)
    if tap == 0:
        amount, keep = RATE, column >= RATE
    else:
        amount, keep = width - RATE, column < width - RATE
    return jnp.stack(
        [jnp.where(keep, pltpu.roll(x[r], amount, 0), 0.0) for r in range(rows)]
    )


def fused_kernel(
    n, rows, width, chans, outs,
    feat_ref, scale_ref, shift_ref, w_hbm, cot_ref,
    branch_ref, fgrad_ref, wgrad_ref,
    w_ref, act_ref, send_ref, all_act, all_cot, cot_sh, part_ref, got_ref,
    w_sem, act_send, act_recv, cot_send, cot_recv, part_send, part_recv,
):
    me = lax.axis_index("rows")
    distance = RATE // rows
    spots = rows * width
    part_chans = chans // n

    def shifted(x, tap):
        return col_shift(x.reshape(rows, width, x.shape[1]), tap).reshape(x.shape)

    def w_copy(tap):
        return pltpu.make_async_copy(w_hbm.at[tap], w_ref.at[tap], w_sem.at[tap])

    for tap in (0, 2, 1):
        w_copy(tap).start()

    barrier = pltpu.get_barrier_semaphore()

    @pl.loop(1, n)
    def _(k):
        pl.semaphore_signal(
            barrier, inc=1, device_id={"rows": lax.rem(me + k, n)},
            device_id_type=pl.DeviceIdType.MESH,
        )

    def cot_copy(peer, source):
        return pltpu.make_async_remote_copy(
            src_ref=cot_ref, dst_ref=all_cot.at[source],
            send_sem=cot_send.at[peer], recv_sem=cot_recv.at[source],
            device_id={"rows": peer}, device_id_type=pl.DeviceIdType.MESH,
        )

    def act_copy(peer, source):
        return pltpu.make_async_remote_copy(
            src_ref=send_ref.at[peer], dst_ref=all_act.at[source],
            send_sem=act_send.at[peer], recv_sem=act_recv.at[source],
            device_id={"rows": peer}, device_id_type=pl.DeviceIdType.MESH,
        )

    def part_copy(tap):
        return pltpu.make_async_remote_copy(
            src_ref=part_ref.at[tap], dst_ref=got_ref.at[tap],
            send_sem=part_send.at[tap], recv_sem=part_recv.at[tap],
            device_id={"rows": jnp.clip(me - distance * (tap - 1), 0, n - 1)},
            device_id_type=pl.DeviceIdType.MESH,
        )

    def inside(index):
        return jnp.logical_and(index >= 0, index < n)

    all_cot[me] = cot_ref[...]

    @pl.loop(0, n)
    def _(k):
        cols = pl.ds(pl.multiple_of(k * part_chans, part_chans), part_chans)
        pre = feat_ref[:, cols].astype(F32) * scale_ref[:, cols] + shift_ref[:, cols]
        act = jnp.maximum(pre, 0.0).astype(BF16)
        act_ref[:, cols] = act
        send_ref[k] = act

    all_act[me] = send_ref[me]

    pl.semaphore_wait(barrier, n - 1)

    @pl.loop(1, n)
    def _(k):
        cot_copy(lax.rem(me + k, n), me).start()

    @pl.loop(1, n)
    def _(k):
        act_copy(lax.rem(me + k, n), me).start()

    @pl.loop(0, 3)
    def _(q):
        tap = lax.rem(2 * q, 3)
        w_copy(tap).wait()
        total = jnp.zeros((spots, outs), F32)
        for j in range(3):
            total = total + shifted(
                jnp.dot(act_ref[...], w_ref[tap, j], preferred_element_type=F32), j
            )
        part_ref[tap] = total

        @pl.when(jnp.logical_and(tap != 1, inside(me - distance * (tap - 1))))
        def _():
            part_copy(tap).start()

    @pl.loop(1, n)
    def _(k):
        source = lax.rem(me + n - k, n)
        cot_copy(source, source).wait_recv()

    for i in range(3):
        source = me - distance * (i - 1)
        block = all_cot[jnp.clip(source, 0, n - 1)].astype(F32)
        block = jnp.where(inside(source), block, 0.0)
        for j in range(3):
            cot_sh[3 * i + j] = shifted(block, 2 - j).astype(BF16)

    step = 256

    @pl.loop(0, chans // step)
    def _(b):
        cols = pl.ds(pl.multiple_of(b * step, step), step)
        total = jnp.zeros((spots, step), F32)
        for i in range(3):
            for j in range(3):
                total = total + lax.dot_general(
                    cot_sh[3 * i + j], w_ref[i, j, cols, :],
                    (((1,), (1,)), ((), ())), preferred_element_type=F32,
                )
        scale = scale_ref[:, cols]
        pre = feat_ref[:, cols].astype(F32) * scale + shift_ref[:, cols]
        rounded = total.astype(BF16).astype(F32)
        fgrad_ref[:, cols] = (scale * jnp.where(pre > 0, rounded, 0.0)).astype(BF16)

    wgrad_ref[...] = jnp.zeros_like(wgrad_ref)

    @pl.loop(0, n)
    def _(k):
        source = lax.rem(me + n - k, n)

        @pl.when(k > 0)
        def _():
            act_copy(source, source).wait_recv()

        block = all_act[source].astype(F32)
        lhs = jnp.concatenate([shifted(block, j).astype(BF16) for j in range(3)], axis=1)
        for i in range(3):
            other = source - distance * (i - 1)

            @pl.when(inside(other))
            def _():
                wgrad_ref[i] += lax.dot_general(
                    lhs, all_cot[other], (((0,), (0,)), ((), ())),
                    preferred_element_type=F32,
                )

    branch = part_ref[1]
    branch_ref[...] = branch.astype(BF16)
    for tap in (0, 2):

        @pl.when(inside(me + distance * (tap - 1)))
        def _():
            part_copy(tap).wait_recv()

        @pl.when(jnp.logical_not(inside(me + distance * (tap - 1))))
        def _():
            got_ref[tap] = jnp.zeros((spots, outs), F32)

    branch_ref[...] = (part_ref[1] + got_ref[0] + got_ref[2]).astype(BF16)

    for tap in (0, 2):

        @pl.when(inside(me - distance * (tap - 1)))
        def _():
            part_copy(tap).wait_send()

    @pl.loop(1, n)
    def _(k):
        peer = lax.rem(me + k, n)
        cot_copy(peer, me).wait_send()
        act_copy(peer, me).wait_send()


def per_device_fused(features, bn_scale, bn_shift, atrous_weight, cotangent):
    rows, width, chans = features.shape
    outs = cotangent.shape[2]
    n = lax.axis_size("rows")
    spots = rows * width
    part = chans // n
    vmem = pl.BlockSpec(memory_space=pltpu.VMEM)
    flops = 2 * 27 * spots * chans * outs
    dma = pltpu.SemaphoreType.DMA
    branch, fgrad, wgrad = pl.pallas_call(
        functools.partial(fused_kernel, n, rows, width, chans, outs),
        out_shape=(
            jax.ShapeDtypeStruct((spots, outs), BF16),
            jax.ShapeDtypeStruct((spots, chans), BF16),
            jax.ShapeDtypeStruct((3, 3 * part, outs), F32),
        ),
        in_specs=[vmem, vmem, vmem, pl.BlockSpec(memory_space=pl.ANY), vmem],
        out_specs=(vmem, vmem, vmem),
        scratch_shapes=[
            pltpu.VMEM(atrous_weight.shape, BF16),
            pltpu.VMEM((spots, chans), BF16),
            pltpu.VMEM((n, spots, part), BF16),
            pltpu.VMEM((n, spots, part), BF16),
            pltpu.VMEM((n, spots, outs), BF16),
            pltpu.VMEM((9, spots, outs), BF16),
            pltpu.VMEM((3, spots, outs), F32),
            pltpu.VMEM((3, spots, outs), F32),
            dma((3,)),
            dma((n,)),
            dma((n,)),
            dma((n,)),
            dma((n,)),
            dma((3,)),
            dma((3,)),
        ],
        compiler_params=pltpu.CompilerParams(
            collective_id=0, has_side_effects=True, vmem_limit_bytes=50 * 2**20
        ),
        cost_estimate=pl.CostEstimate(
            flops=flops, bytes_accessed=14 * 2**20, transcendentals=0
        ),
    )(
        features.reshape(spots, chans),
        bn_scale.reshape(1, chans),
        bn_shift.reshape(1, chans),
        atrous_weight,
        cotangent.reshape(spots, outs),
    )
    return (
        branch.reshape(rows, width, outs),
        fgrad.reshape(rows, width, chans),
        wgrad.reshape(3, 3, part, outs),
    )


def from_behind(array, axis, by):
    devices = lax.axis_size(axis)
    pairs = [(i, i + by) for i in range(devices) if 0 <= i + by < devices]
    return lax.ppermute(array, axis, pairs)


def branch_forward(blocks, atrous_weight, width):
    total = jnp.zeros(blocks[1].shape[:2] + (atrous_weight.shape[3],), jnp.float32)
    for row_tap in range(3):
        padded = jnp.pad(blocks[row_tap], ((0, 0), (RATE, RATE), (0, 0)))
        for col_tap in range(3):
            window = padded[:, RATE * col_tap : RATE * col_tap + width]
            total = total + jnp.einsum(
                "hwc,ck->hwk",
                window,
                atrous_weight[row_tap, col_tap],
                preferred_element_type=jnp.float32,
            )
    return total


def spatial_act_grad(blocks, atrous_weight, width):
    total = jnp.zeros(blocks[1].shape[:2] + (atrous_weight.shape[2],), jnp.float32)
    for row_tap in range(3):
        padded = jnp.pad(blocks[row_tap], ((0, 0), (RATE, RATE), (0, 0)))
        for col_tap in range(3):
            window = padded[:, RATE * (2 - col_tap) : RATE * (2 - col_tap) + width]
            total = total + jnp.einsum(
                "hwk,ck->hwc",
                window,
                atrous_weight[row_tap, col_tap],
                preferred_element_type=jnp.float32,
            )
    return total


def spatial_kernel_terms(blocks, cotangent, width):
    kernel_rows = []
    for row_tap in range(3):
        padded = jnp.pad(blocks[row_tap], ((0, 0), (RATE, RATE), (0, 0)))
        kernel_cols = []
        for col_tap in range(3):
            window = padded[:, RATE * col_tap : RATE * col_tap + width]
            kernel_cols.append(
                jnp.einsum("hwc,hwk->ck", window, cotangent, preferred_element_type=jnp.float32)
            )
        kernel_rows.append(jnp.stack(kernel_cols))
    return jnp.stack(kernel_rows)


def per_device_plain(features, bn_scale, bn_shift, atrous_weight, cotangent):
    local_rows, width, chans = features.shape
    distance = RATE // local_rows
    pre_act = features.astype(jnp.float32) * bn_scale + bn_shift
    activated = jnp.maximum(pre_act, 0.0).astype(jnp.bfloat16)
    act_above, cot_above = from_behind((activated, cotangent), "rows", distance)
    act_below, cot_below = from_behind((activated, cotangent), "rows", -distance)
    blocks = (act_above, activated, act_below)
    branch = branch_forward(blocks, atrous_weight, width)
    act_grad = spatial_act_grad((cot_below, cotangent, cot_above), atrous_weight, width)
    terms = spatial_kernel_terms(blocks, cotangent, width)
    weight_grad = lax.psum_scatter(terms, "rows", scatter_dimension=2, tiled=True)
    branch_out = branch.astype(jnp.bfloat16)
    rounded = lax.optimization_barrier(act_grad.astype(jnp.bfloat16)).astype(jnp.float32)
    feature_grad = (bn_scale * jnp.where(pre_act > 0, rounded, 0.0)).astype(jnp.bfloat16)
    return (branch_out, feature_grad, weight_grad)


def per_device(features, *others):
    rows, width, chans = features.shape
    fits = (
        chans == LANES * lax.axis_size("rows")
        and RATE % rows == 0
        and width % 16 == 0
        and width > RATE
        and others[-1].shape[2] % LANES == 0
    )
    return (per_device_fused if fits else per_device_plain)(features, *others)


def solution(mesh):
    return jax.shard_map(
        per_device,
        mesh=mesh,
        in_specs=(
            P(("crops", "rows"), None, None),
            P(),
            P(),
            P(),
            P(("crops", "rows"), None, None),
        ),
        out_specs=(
            P(("crops", "rows"), None, None),
            P(("crops", "rows"), None, None),
            P("crops", None, "rows", None),
        ),
        check_vma=False,
    )
```

```python
import functools

import jax
import jax.numpy as jnp
from jax import lax
from jax.experimental import pallas as pl
from jax.experimental.pallas import tpu as pltpu
from jax.sharding import PartitionSpec as P

RATE = 12
LANES = 128
BF16 = jnp.bfloat16
F32 = jnp.float32


def col_shift(x, tap):
    if tap == 1:
        return x
    rows, width, _ = x.shape
    column = lax.broadcasted_iota(jnp.int32, x.shape[1:], 0)
    if tap == 0:
        amount, keep = RATE, column >= RATE
    else:
        amount, keep = width - RATE, column < width - RATE
    return jnp.stack(
        [jnp.where(keep, pltpu.roll(x[r], amount, 0), 0.0) for r in range(rows)]
    )


def fused_kernel(
    n, rows, width, chans, outs,
    feat_hbm, scale_ref, shift_ref, w_hbm, cot_hbm,
    branch_ref, fgrad_ref, wgrad_ref,
    w_ref, feat_ref, act_ref, send_ref, all_act, all_cot, cot_sh, own_ref, part_ref, got_ref,
    w_sem, feat_sem, act_send, act_recv, cot_send, cot_recv, part_send, part_recv,
):
    me = lax.axis_index("rows")
    distance = RATE // rows
    spots = rows * width
    part_chans = chans // n
    slow = n // 4
    mine, low = me // 4, lax.rem(me, 4)
    other_mid = lax.rem(low + 2, 4)
    other_core = low + 1 - 2 * lax.rem(low, 2)

    def shifted(x, tap):
        return col_shift(x.reshape(rows, width, x.shape[1]), tap).reshape(x.shape)

    def w_copy(tap):
        return pltpu.make_async_copy(w_hbm.at[tap], w_ref.at[tap], w_sem.at[tap])

    feat_copy = pltpu.make_async_copy(feat_hbm, feat_ref, feat_sem.at[0])
    own_cot_copy = pltpu.make_async_copy(cot_hbm, all_cot.at[me], feat_sem.at[1])
    feat_copy.start()
    own_cot_copy.start()
    for tap in (0, 2, 1):
        w_copy(tap).start()

    barrier = pltpu.get_barrier_semaphore()

    @pl.loop(1, n)
    def _(k):
        pl.semaphore_signal(
            barrier, inc=1, device_id={"rows": lax.rem(me + k, n)},
            device_id_type=pl.DeviceIdType.MESH,
        )

    def cot_copy(way, source):
        peer = (
            jnp.minimum(me + 4, n - 4 + low),
            jnp.maximum(me - 4, low),
            4 * mine + other_mid,
            4 * mine + other_core,
        )[way]
        return pltpu.make_async_remote_copy(
            src_ref=all_cot.at[source], dst_ref=all_cot.at[source],
            send_sem=cot_send.at[way, source], recv_sem=cot_recv.at[source],
            device_id={"rows": peer}, device_id_type=pl.DeviceIdType.MESH,
        )

    def take_slow(hops):
        for sign in (1, -1):
            row = mine - sign * hops
            source = 4 * row + low

            @pl.when(jnp.logical_and(row >= 0, row < slow))
            def _():
                onward = 0 if sign == 1 else 1
                cot_copy(onward, source).wait_recv()

                @pl.when(jnp.logical_and(mine + sign >= 0, mine + sign < slow))
                def _():
                    cot_copy(onward, source).start()

                cot_copy(2, source).start()
                cot_copy(3, source).start()

    def act_copy(peer, source):
        return pltpu.make_async_remote_copy(
            src_ref=send_ref.at[peer], dst_ref=all_act.at[source],
            send_sem=act_send.at[peer], recv_sem=act_recv.at[source],
            device_id={"rows": peer}, device_id_type=pl.DeviceIdType.MESH,
        )

    def part_copy(tap):
        return pltpu.make_async_remote_copy(
            src_ref=part_ref.at[tap], dst_ref=got_ref.at[tap],
            send_sem=part_send.at[tap], recv_sem=part_recv.at[tap],
            device_id={"rows": jnp.clip(me - distance * (tap - 1), 0, n - 1)},
            device_id_type=pl.DeviceIdType.MESH,
        )

    def inside(index):
        return jnp.logical_and(index >= 0, index < n)

    feat_copy.wait()

    @pl.loop(0, n)
    def _(k):
        cols = pl.ds(pl.multiple_of(k * part_chans, part_chans), part_chans)
        pre = feat_ref[:, cols].astype(F32) * scale_ref[:, cols] + shift_ref[:, cols]
        act = jnp.maximum(pre, 0.0).astype(BF16)
        act_ref[:, cols] = act
        send_ref[k] = act

    all_act[me] = send_ref[me]

    pl.semaphore_wait(barrier, n - 1)

    own_cot_copy.wait()

    @pl.when(mine + 1 < slow)
    def _():
        cot_copy(0, me).start()

    @pl.when(mine > 0)
    def _():
        cot_copy(1, me).start()

    cot_copy(2, me).start()
    cot_copy(3, me).start()

    @pl.loop(1, n)
    def _(k):
        act_copy(lax.rem(me + k, n), me).start()

    @pl.loop(0, 3)
    def _(q):
        tap = lax.rem(2 * q, 3)
        take_slow(q + 1)
        w_copy(tap).wait()
        total = jnp.zeros((spots, outs), F32)
        for j in range(3):
            total = total + shifted(
                jnp.dot(act_ref[...], w_ref[tap, j], preferred_element_type=F32), j
            )
        part_ref[tap] = total.astype(BF16)

        @pl.when(tap == 1)
        def _():
            own_ref[...] = total

        @pl.when(jnp.logical_and(tap != 1, inside(me - distance * (tap - 1))))
        def _():
            part_copy(tap).start()

    @pl.loop(0, slow)
    def _(k):
        source = 4 * k + other_mid
        cot_copy(2, source).wait_recv()
        cot_copy(3, source).start()

    @pl.loop(0, slow)
    def _(k):
        cot_copy(3, 4 * k + other_core).wait_recv()
        cot_copy(3, 4 * k + lax.rem(other_core + 2, 4)).wait_recv()

    for i in range(3):
        source = me - distance * (i - 1)
        block = all_cot[jnp.clip(source, 0, n - 1)].astype(F32)
        block = jnp.where(inside(source), block, 0.0)
        for j in range(3):
            cot_sh[3 * i + j] = shifted(block, 2 - j).astype(BF16)

    step = 256

    @pl.loop(0, chans // step)
    def _(b):
        cols = pl.ds(pl.multiple_of(b * step, step), step)
        total = jnp.zeros((spots, step), F32)
        for i in range(3):
            for j in range(3):
                total = total + lax.dot_general(
                    cot_sh[3 * i + j], w_ref[i, j, cols, :],
                    (((1,), (1,)), ((), ())), preferred_element_type=F32,
                )
        scale = scale_ref[:, cols]
        pre = feat_ref[:, cols].astype(F32) * scale + shift_ref[:, cols]
        rounded = total.astype(BF16).astype(F32)
        fgrad_ref[:, cols] = (scale * jnp.where(pre > 0, rounded, 0.0)).astype(BF16)

    wgrad_ref[...] = jnp.zeros_like(wgrad_ref)

    @pl.loop(0, n)
    def _(k):
        source = lax.rem(me + n - k, n)

        @pl.when(k > 0)
        def _():
            act_copy(source, source).wait_recv()

        block = all_act[source].astype(F32)
        lhs = jnp.concatenate([shifted(block, j).astype(BF16) for j in range(3)], axis=1)
        for i in range(3):
            other = source - distance * (i - 1)

            @pl.when(inside(other))
            def _():
                wgrad_ref[i] += lax.dot_general(
                    lhs, all_cot[other], (((0,), (0,)), ((), ())),
                    preferred_element_type=F32,
                )

    for tap in (0, 2):

        @pl.when(inside(me + distance * (tap - 1)))
        def _():
            part_copy(tap).wait_recv()

        @pl.when(jnp.logical_not(inside(me + distance * (tap - 1))))
        def _():
            got_ref[tap] = jnp.zeros((spots, outs), BF16)

    branch_ref[...] = (own_ref[...] + got_ref[0].astype(F32) + got_ref[2].astype(F32)).astype(BF16)

    for tap in (0, 2):

        @pl.when(inside(me - distance * (tap - 1)))
        def _():
            part_copy(tap).wait_send()

    @pl.loop(1, n)
    def _(k):
        peer = lax.rem(me + k, n)
        act_copy(peer, me).wait_send()

    @pl.loop(0, slow)
    def _(k):
        source = 4 * k + low

        @pl.when(jnp.logical_and(k <= mine, mine + 1 < slow))
        def _():
            cot_copy(0, source).wait_send()

        @pl.when(jnp.logical_and(k >= mine, mine > 0))
        def _():
            cot_copy(1, source).wait_send()

        cot_copy(2, source).wait_send()
        cot_copy(3, source).wait_send()
        cot_copy(3, 4 * k + other_mid).wait_send()


def per_device_fused(features, bn_scale, bn_shift, atrous_weight, cotangent):
    rows, width, chans = features.shape
    outs = cotangent.shape[2]
    n = lax.axis_size("rows")
    spots = rows * width
    part = chans // n
    vmem = pl.BlockSpec(memory_space=pltpu.VMEM)
    anywhere = pl.BlockSpec(memory_space=pl.ANY)
    flops = 2 * 27 * spots * chans * outs
    dma = pltpu.SemaphoreType.DMA
    branch, fgrad, wgrad = pl.pallas_call(
        functools.partial(fused_kernel, n, rows, width, chans, outs),
        out_shape=(
            jax.ShapeDtypeStruct((spots, outs), BF16),
            jax.ShapeDtypeStruct((spots, chans), BF16),
            jax.ShapeDtypeStruct((3, 3 * part, outs), F32),
        ),
        in_specs=[anywhere, vmem, vmem, anywhere, anywhere],
        out_specs=(vmem, vmem, vmem),
        scratch_shapes=[
            pltpu.VMEM(atrous_weight.shape, BF16),
            pltpu.VMEM((spots, chans), BF16),
            pltpu.VMEM((spots, chans), BF16),
            pltpu.VMEM((n, spots, part), BF16),
            pltpu.VMEM((n, spots, part), BF16),
            pltpu.VMEM((n, spots, outs), BF16),
            pltpu.VMEM((9, spots, outs), BF16),
            pltpu.VMEM((spots, outs), F32),
            pltpu.VMEM((3, spots, outs), BF16),
            pltpu.VMEM((3, spots, outs), BF16),
            dma((3,)),
            dma((2,)),
            dma((n,)),
            dma((n,)),
            dma((4, n)),
            dma((n,)),
            dma((3,)),
            dma((3,)),
        ],
        compiler_params=pltpu.CompilerParams(
            collective_id=0, has_side_effects=True, vmem_limit_bytes=50 * 2**20
        ),
        cost_estimate=pl.CostEstimate(
            flops=flops, bytes_accessed=14 * 2**20, transcendentals=0
        ),
    )(
        features.reshape(spots, chans),
        bn_scale.reshape(1, chans),
        bn_shift.reshape(1, chans),
        atrous_weight,
        cotangent.reshape(spots, outs),
    )
    return (
        branch.reshape(rows, width, outs),
        fgrad.reshape(rows, width, chans),
        wgrad.reshape(3, 3, part, outs),
    )


def from_behind(array, axis, by):
    devices = lax.axis_size(axis)
    pairs = [(i, i + by) for i in range(devices) if 0 <= i + by < devices]
    return lax.ppermute(array, axis, pairs)


def branch_forward(blocks, atrous_weight, width):
    total = jnp.zeros(blocks[1].shape[:2] + (atrous_weight.shape[3],), jnp.float32)
    for row_tap in range(3):
        padded = jnp.pad(blocks[row_tap], ((0, 0), (RATE, RATE), (0, 0)))
        for col_tap in range(3):
            window = padded[:, RATE * col_tap : RATE * col_tap + width]
            total = total + jnp.einsum(
                "hwc,ck->hwk",
                window,
                atrous_weight[row_tap, col_tap],
                preferred_element_type=jnp.float32,
            )
    return total


def spatial_act_grad(blocks, atrous_weight, width):
    total = jnp.zeros(blocks[1].shape[:2] + (atrous_weight.shape[2],), jnp.float32)
    for row_tap in range(3):
        padded = jnp.pad(blocks[row_tap], ((0, 0), (RATE, RATE), (0, 0)))
        for col_tap in range(3):
            window = padded[:, RATE * (2 - col_tap) : RATE * (2 - col_tap) + width]
            total = total + jnp.einsum(
                "hwk,ck->hwc",
                window,
                atrous_weight[row_tap, col_tap],
                preferred_element_type=jnp.float32,
            )
    return total


def spatial_kernel_terms(blocks, cotangent, width):
    kernel_rows = []
    for row_tap in range(3):
        padded = jnp.pad(blocks[row_tap], ((0, 0), (RATE, RATE), (0, 0)))
        kernel_cols = []
        for col_tap in range(3):
            window = padded[:, RATE * col_tap : RATE * col_tap + width]
            kernel_cols.append(
                jnp.einsum("hwc,hwk->ck", window, cotangent, preferred_element_type=jnp.float32)
            )
        kernel_rows.append(jnp.stack(kernel_cols))
    return jnp.stack(kernel_rows)


def per_device_plain(features, bn_scale, bn_shift, atrous_weight, cotangent):
    local_rows, width, chans = features.shape
    distance = RATE // local_rows
    pre_act = features.astype(jnp.float32) * bn_scale + bn_shift
    activated = jnp.maximum(pre_act, 0.0).astype(jnp.bfloat16)
    act_above, cot_above = from_behind((activated, cotangent), "rows", distance)
    act_below, cot_below = from_behind((activated, cotangent), "rows", -distance)
    blocks = (act_above, activated, act_below)
    branch = branch_forward(blocks, atrous_weight, width)
    act_grad = spatial_act_grad((cot_below, cotangent, cot_above), atrous_weight, width)
    terms = spatial_kernel_terms(blocks, cotangent, width)
    weight_grad = lax.psum_scatter(terms, "rows", scatter_dimension=2, tiled=True)
    branch_out = branch.astype(jnp.bfloat16)
    rounded = lax.optimization_barrier(act_grad.astype(jnp.bfloat16)).astype(jnp.float32)
    feature_grad = (bn_scale * jnp.where(pre_act > 0, rounded, 0.0)).astype(jnp.bfloat16)
    return (branch_out, feature_grad, weight_grad)


def per_device(features, *others):
    rows, width, chans = features.shape
    fits = (
        lax.axis_size("rows") == 16
        and chans == 16 * LANES
        and RATE % rows == 0
        and width % 16 == 0
        and width > RATE
        and others[-1].shape[2] % LANES == 0
    )
    return (per_device_fused if fits else per_device_plain)(features, *others)


def solution(mesh):
    return jax.shard_map(
        per_device,
        mesh=mesh,
        in_specs=(
            P(("crops", "rows"), None, None),
            P(),
            P(),
            P(),
            P(("crops", "rows"), None, None),
        ),
        out_specs=(
            P(("crops", "rows"), None, None),
            P(("crops", "rows"), None, None),
            P("crops", None, "rows", None),
        ),
        check_vma=False,
    )
```

```python
import functools

import jax
import jax.numpy as jnp
from jax import lax
from jax.experimental import pallas as pl
from jax.experimental.pallas import tpu as pltpu
from jax.sharding import PartitionSpec as P

RATE = 12
LANES = 128
BF16 = jnp.bfloat16
F32 = jnp.float32


def col_shift(x, tap):
    if tap == 1:
        return x
    rows, width, _ = x.shape
    column = lax.broadcasted_iota(jnp.int32, x.shape[1:], 0)
    if tap == 0:
        amount, keep = RATE, column >= RATE
    else:
        amount, keep = width - RATE, column < width - RATE
    return jnp.stack(
        [jnp.where(keep, pltpu.roll(x[r], amount, 0), 0.0) for r in range(rows)]
    )


def fused_kernel(
    n, rows, width, chans, outs,
    feat_hbm, scale_ref, shift_ref, w_hbm, cot_hbm,
    branch_ref, fgrad_ref, wgrad_ref,
    w_ref, feat_ref, act_ref, send_ref, all_act, all_cot, cot_sh, own_ref, part_ref, got_ref,
    w_sem, feat_sem, act_send, act_recv, cot_send, cot_recv, part_send, part_recv,
):
    me = lax.axis_index("rows")
    distance = RATE // rows
    spots = rows * width
    part_chans = chans // n
    slow = n // 4
    mine, low = me // 4, lax.rem(me, 4)
    other_mid = lax.rem(low + 2, 4)
    other_core = low + 1 - 2 * lax.rem(low, 2)

    def shifted(x, tap):
        return col_shift(x.reshape(rows, width, x.shape[1]), tap).reshape(x.shape)

    def w_copy(tap):
        return pltpu.make_async_copy(w_hbm.at[tap], w_ref.at[tap], w_sem.at[tap])

    feat_copy = pltpu.make_async_copy(feat_hbm, feat_ref, feat_sem.at[0])
    own_cot_copy = pltpu.make_async_copy(cot_hbm, all_cot.at[me], feat_sem.at[1])
    feat_copy.start()
    own_cot_copy.start()
    for tap in (0, 2, 1):
        w_copy(tap).start()

    barrier = pltpu.get_barrier_semaphore()

    @pl.loop(1, n)
    def _(k):
        pl.semaphore_signal(
            barrier, inc=1, device_id={"rows": lax.rem(me + k, n)},
            device_id_type=pl.DeviceIdType.MESH,
        )

    def cot_copy(way, source):
        peer = (
            jnp.minimum(me + 4, n - 4 + low),
            jnp.maximum(me - 4, low),
            4 * mine + other_mid,
            4 * mine + other_core,
        )[way]
        return pltpu.make_async_remote_copy(
            src_ref=all_cot.at[source], dst_ref=all_cot.at[source],
            send_sem=cot_send.at[way, source], recv_sem=cot_recv.at[source],
            device_id={"rows": peer}, device_id_type=pl.DeviceIdType.MESH,
        )

    def take_slow(hops):
        for sign in (1, -1):
            row = mine - sign * hops
            source = 4 * row + low

            @pl.when(jnp.logical_and(row >= 0, row < slow))
            def _():
                onward = 0 if sign == 1 else 1
                cot_copy(onward, source).wait_recv()

                @pl.when(jnp.logical_and(mine + sign >= 0, mine + sign < slow))
                def _():
                    cot_copy(onward, source).start()

                cot_copy(2, source).start()
                cot_copy(3, source).start()

    def act_copy(peer, source):
        return pltpu.make_async_remote_copy(
            src_ref=send_ref.at[peer], dst_ref=all_act.at[source],
            send_sem=act_send.at[peer], recv_sem=act_recv.at[source],
            device_id={"rows": peer}, device_id_type=pl.DeviceIdType.MESH,
        )

    def part_copy(tap):
        return pltpu.make_async_remote_copy(
            src_ref=part_ref.at[tap], dst_ref=got_ref.at[tap],
            send_sem=part_send.at[tap], recv_sem=part_recv.at[tap],
            device_id={"rows": jnp.clip(me - distance * (tap - 1), 0, n - 1)},
            device_id_type=pl.DeviceIdType.MESH,
        )

    def inside(index):
        return jnp.logical_and(index >= 0, index < n)

    feat_copy.wait()

    @pl.loop(0, n)
    def _(k):
        cols = pl.ds(pl.multiple_of(k * part_chans, part_chans), part_chans)
        pre = feat_ref[:, cols].astype(F32) * scale_ref[:, cols] + shift_ref[:, cols]
        act = jnp.maximum(pre, 0.0).astype(BF16)
        act_ref[:, cols] = act
        send_ref[k] = act

    all_act[me] = send_ref[me]

    pl.semaphore_wait(barrier, n - 1)

    own_cot_copy.wait()

    @pl.when(mine + 1 < slow)
    def _():
        cot_copy(0, me).start()

    @pl.when(mine > 0)
    def _():
        cot_copy(1, me).start()

    cot_copy(2, me).start()
    cot_copy(3, me).start()

    def send_acts(first, count):
        @pl.loop(0, count)
        def _(t):
            act_copy(lax.rem(me + first + t, n), me).start()

    send_acts(1, 1)

    @pl.loop(0, 3)
    def _(q):
        tap = lax.rem(2 * q, 3)
        take_slow(q + 1)
        send_acts(2 + 1 * q, 1)
        w_copy(tap).wait()
        total = jnp.zeros((spots, outs), F32)
        for j in range(3):
            total = total + shifted(
                jnp.dot(act_ref[...], w_ref[tap, j], preferred_element_type=F32), j
            )
        part_ref[tap] = total.astype(BF16)

        @pl.when(tap == 1)
        def _():
            own_ref[...] = total

        @pl.when(jnp.logical_and(tap != 1, inside(me - distance * (tap - 1))))
        def _():
            part_copy(tap).start()

    @pl.loop(0, slow)
    def _(k):
        source = 4 * k + other_mid
        cot_copy(2, source).wait_recv()
        cot_copy(3, source).start()

    send_acts(5, 4)

    @pl.loop(0, slow)
    def _(k):
        cot_copy(3, 4 * k + other_core).wait_recv()
        cot_copy(3, 4 * k + lax.rem(other_core + 2, 4)).wait_recv()

    send_acts(9, 7)

    for i in range(3):
        source = me - distance * (i - 1)
        block = all_cot[jnp.clip(source, 0, n - 1)].astype(F32)
        block = jnp.where(inside(source), block, 0.0)
        for j in range(3):
            cot_sh[3 * i + j] = shifted(block, 2 - j).astype(BF16)

    step = 256

    @pl.loop(0, chans // step)
    def _(b):
        cols = pl.ds(pl.multiple_of(b * step, step), step)
        total = jnp.zeros((spots, step), F32)
        for i in range(3):
            for j in range(3):
                total = total + lax.dot_general(
                    cot_sh[3 * i + j], w_ref[i, j, cols, :],
                    (((1,), (1,)), ((), ())), preferred_element_type=F32,
                )
        scale = scale_ref[:, cols]
        pre = feat_ref[:, cols].astype(F32) * scale + shift_ref[:, cols]
        rounded = total.astype(BF16).astype(F32)
        fgrad_ref[:, cols] = (scale * jnp.where(pre > 0, rounded, 0.0)).astype(BF16)

    wgrad_ref[...] = jnp.zeros_like(wgrad_ref)

    @pl.loop(0, n)
    def _(k):
        source = lax.rem(me + n - k, n)

        @pl.when(k > 0)
        def _():
            act_copy(source, source).wait_recv()

        block = all_act[source].astype(F32)
        lhs = jnp.concatenate([shifted(block, j).astype(BF16) for j in range(3)], axis=1)
        for i in range(3):
            other = source - distance * (i - 1)

            @pl.when(inside(other))
            def _():
                wgrad_ref[i] += lax.dot_general(
                    lhs, all_cot[other], (((0,), (0,)), ((), ())),
                    preferred_element_type=F32,
                )

    for tap in (0, 2):

        @pl.when(inside(me + distance * (tap - 1)))
        def _():
            part_copy(tap).wait_recv()

        @pl.when(jnp.logical_not(inside(me + distance * (tap - 1))))
        def _():
            got_ref[tap] = jnp.zeros((spots, outs), BF16)

    branch_ref[...] = (own_ref[...] + got_ref[0].astype(F32) + got_ref[2].astype(F32)).astype(BF16)

    for tap in (0, 2):

        @pl.when(inside(me - distance * (tap - 1)))
        def _():
            part_copy(tap).wait_send()

    @pl.loop(1, n)
    def _(k):
        peer = lax.rem(me + k, n)
        act_copy(peer, me).wait_send()

    @pl.loop(0, slow)
    def _(k):
        source = 4 * k + low

        @pl.when(jnp.logical_and(k <= mine, mine + 1 < slow))
        def _():
            cot_copy(0, source).wait_send()

        @pl.when(jnp.logical_and(k >= mine, mine > 0))
        def _():
            cot_copy(1, source).wait_send()

        cot_copy(2, source).wait_send()
        cot_copy(3, source).wait_send()
        cot_copy(3, 4 * k + other_mid).wait_send()


def per_device_fused(features, bn_scale, bn_shift, atrous_weight, cotangent):
    rows, width, chans = features.shape
    outs = cotangent.shape[2]
    n = lax.axis_size("rows")
    spots = rows * width
    part = chans // n
    vmem = pl.BlockSpec(memory_space=pltpu.VMEM)
    anywhere = pl.BlockSpec(memory_space=pl.ANY)
    flops = 2 * 27 * spots * chans * outs
    dma = pltpu.SemaphoreType.DMA
    branch, fgrad, wgrad = pl.pallas_call(
        functools.partial(fused_kernel, n, rows, width, chans, outs),
        out_shape=(
            jax.ShapeDtypeStruct((spots, outs), BF16),
            jax.ShapeDtypeStruct((spots, chans), BF16),
            jax.ShapeDtypeStruct((3, 3 * part, outs), F32),
        ),
        in_specs=[anywhere, vmem, vmem, anywhere, anywhere],
        out_specs=(vmem, vmem, vmem),
        scratch_shapes=[
            pltpu.VMEM(atrous_weight.shape, BF16),
            pltpu.VMEM((spots, chans), BF16),
            pltpu.VMEM((spots, chans), BF16),
            pltpu.VMEM((n, spots, part), BF16),
            pltpu.VMEM((n, spots, part), BF16),
            pltpu.VMEM((n, spots, outs), BF16),
            pltpu.VMEM((9, spots, outs), BF16),
            pltpu.VMEM((spots, outs), F32),
            pltpu.VMEM((3, spots, outs), BF16),
            pltpu.VMEM((3, spots, outs), BF16),
            dma((3,)),
            dma((2,)),
            dma((n,)),
            dma((n,)),
            dma((4, n)),
            dma((n,)),
            dma((3,)),
            dma((3,)),
        ],
        compiler_params=pltpu.CompilerParams(
            collective_id=0, has_side_effects=True, vmem_limit_bytes=50 * 2**20
        ),
        cost_estimate=pl.CostEstimate(
            flops=flops, bytes_accessed=14 * 2**20, transcendentals=0
        ),
    )(
        features.reshape(spots, chans),
        bn_scale.reshape(1, chans),
        bn_shift.reshape(1, chans),
        atrous_weight,
        cotangent.reshape(spots, outs),
    )
    return (
        branch.reshape(rows, width, outs),
        fgrad.reshape(rows, width, chans),
        wgrad.reshape(3, 3, part, outs),
    )


def from_behind(array, axis, by):
    devices = lax.axis_size(axis)
    pairs = [(i, i + by) for i in range(devices) if 0 <= i + by < devices]
    return lax.ppermute(array, axis, pairs)


def branch_forward(blocks, atrous_weight, width):
    total = jnp.zeros(blocks[1].shape[:2] + (atrous_weight.shape[3],), jnp.float32)
    for row_tap in range(3):
        padded = jnp.pad(blocks[row_tap], ((0, 0), (RATE, RATE), (0, 0)))
        for col_tap in range(3):
            window = padded[:, RATE * col_tap : RATE * col_tap + width]
            total = total + jnp.einsum(
                "hwc,ck->hwk",
                window,
                atrous_weight[row_tap, col_tap],
                preferred_element_type=jnp.float32,
            )
    return total


def spatial_act_grad(blocks, atrous_weight, width):
    total = jnp.zeros(blocks[1].shape[:2] + (atrous_weight.shape[2],), jnp.float32)
    for row_tap in range(3):
        padded = jnp.pad(blocks[row_tap], ((0, 0), (RATE, RATE), (0, 0)))
        for col_tap in range(3):
            window = padded[:, RATE * (2 - col_tap) : RATE * (2 - col_tap) + width]
            total = total + jnp.einsum(
                "hwk,ck->hwc",
                window,
                atrous_weight[row_tap, col_tap],
                preferred_element_type=jnp.float32,
            )
    return total


def spatial_kernel_terms(blocks, cotangent, width):
    kernel_rows = []
    for row_tap in range(3):
        padded = jnp.pad(blocks[row_tap], ((0, 0), (RATE, RATE), (0, 0)))
        kernel_cols = []
        for col_tap in range(3):
            window = padded[:, RATE * col_tap : RATE * col_tap + width]
            kernel_cols.append(
                jnp.einsum("hwc,hwk->ck", window, cotangent, preferred_element_type=jnp.float32)
            )
        kernel_rows.append(jnp.stack(kernel_cols))
    return jnp.stack(kernel_rows)


def per_device_plain(features, bn_scale, bn_shift, atrous_weight, cotangent):
    local_rows, width, chans = features.shape
    distance = RATE // local_rows
    pre_act = features.astype(jnp.float32) * bn_scale + bn_shift
    activated = jnp.maximum(pre_act, 0.0).astype(jnp.bfloat16)
    act_above, cot_above = from_behind((activated, cotangent), "rows", distance)
    act_below, cot_below = from_behind((activated, cotangent), "rows", -distance)
    blocks = (act_above, activated, act_below)
    branch = branch_forward(blocks, atrous_weight, width)
    act_grad = spatial_act_grad((cot_below, cotangent, cot_above), atrous_weight, width)
    terms = spatial_kernel_terms(blocks, cotangent, width)
    weight_grad = lax.psum_scatter(terms, "rows", scatter_dimension=2, tiled=True)
    branch_out = branch.astype(jnp.bfloat16)
    rounded = lax.optimization_barrier(act_grad.astype(jnp.bfloat16)).astype(jnp.float32)
    feature_grad = (bn_scale * jnp.where(pre_act > 0, rounded, 0.0)).astype(jnp.bfloat16)
    return (branch_out, feature_grad, weight_grad)


def per_device(features, *others):
    rows, width, chans = features.shape
    fits = (
        lax.axis_size("rows") == 16
        and chans == 16 * LANES
        and RATE % rows == 0
        and width % 16 == 0
        and width > RATE
        and others[-1].shape[2] % LANES == 0
    )
    return (per_device_fused if fits else per_device_plain)(features, *others)


def solution(mesh):
    return jax.shard_map(
        per_device,
        mesh=mesh,
        in_specs=(
            P(("crops", "rows"), None, None),
            P(),
            P(),
            P(),
            P(("crops", "rows"), None, None),
        ),
        out_specs=(
            P(("crops", "rows"), None, None),
            P(("crops", "rows"), None, None),
            P("crops", None, "rows", None),
        ),
        check_vma=False,
    )
```

```python
import functools

import jax
import jax.numpy as jnp
from jax import lax
from jax.experimental import pallas as pl
from jax.experimental.pallas import tpu as pltpu
from jax.sharding import PartitionSpec as P

RATE = 12
LANES = 128
BF16 = jnp.bfloat16
F32 = jnp.float32


def col_shift(x, tap):
    if tap == 1:
        return x
    rows, width, _ = x.shape
    column = lax.broadcasted_iota(jnp.int32, x.shape[1:], 0)
    if tap == 0:
        amount, keep = RATE, column >= RATE
    else:
        amount, keep = width - RATE, column < width - RATE
    return jnp.stack(
        [jnp.where(keep, pltpu.roll(x[r], amount, 0), 0.0) for r in range(rows)]
    )


def fused_kernel(
    n, rows, width, chans, outs,
    feat_hbm, scale_ref, shift_ref, w_hbm, cot_hbm,
    branch_ref, fgrad_ref, wgrad_ref,
    w_ref, feat_ref, act_ref, send_ref, all_act, all_cot, cot_sh, own_ref, part_ref, got_ref,
    w_sem, feat_sem, act_send, act_recv, cot_send, cot_recv, part_send, part_recv,
):
    me = lax.axis_index("rows")
    distance = RATE // rows
    spots = rows * width
    part_chans = chans // n
    slow = n // 4
    mine, low = me // 4, lax.rem(me, 4)
    other_mid = lax.rem(low + 2, 4)
    other_core = low + 1 - 2 * lax.rem(low, 2)

    def shifted(x, tap):
        return col_shift(x.reshape(rows, width, x.shape[1]), tap).reshape(x.shape)

    def w_copy(tap):
        return pltpu.make_async_copy(w_hbm.at[tap], w_ref.at[tap], w_sem.at[tap])

    feat_copy = pltpu.make_async_copy(feat_hbm, feat_ref, feat_sem.at[0])
    own_cot_copy = pltpu.make_async_copy(cot_hbm, all_cot.at[me], feat_sem.at[1])
    feat_copy.start()
    own_cot_copy.start()
    for tap in (0, 2, 1):
        w_copy(tap).start()

    barrier = pltpu.get_barrier_semaphore()

    @pl.loop(1, n)
    def _(k):
        pl.semaphore_signal(
            barrier, inc=1, device_id={"rows": lax.rem(me + k, n)},
            device_id_type=pl.DeviceIdType.MESH,
        )

    def cot_copy(way, source):
        peer = (
            jnp.minimum(me + 4, n - 4 + low),
            jnp.maximum(me - 4, low),
            4 * mine + other_mid,
            4 * mine + other_core,
        )[way]
        return pltpu.make_async_remote_copy(
            src_ref=all_cot.at[source], dst_ref=all_cot.at[source],
            send_sem=cot_send.at[way, source], recv_sem=cot_recv.at[source],
            device_id={"rows": peer}, device_id_type=pl.DeviceIdType.MESH,
        )

    def take_slow(hops):
        for sign in (1, -1):
            row = mine - sign * hops
            source = 4 * row + low

            @pl.when(jnp.logical_and(row >= 0, row < slow))
            def _():
                onward = 0 if sign == 1 else 1
                cot_copy(onward, source).wait_recv()

                @pl.when(jnp.logical_and(mine + sign >= 0, mine + sign < slow))
                def _():
                    cot_copy(onward, source).start()

                cot_copy(2, source).start()
                cot_copy(3, source).start()

    def act_copy(peer, source):
        return pltpu.make_async_remote_copy(
            src_ref=send_ref.at[peer], dst_ref=all_act.at[source],
            send_sem=act_send.at[peer], recv_sem=act_recv.at[source],
            device_id={"rows": peer}, device_id_type=pl.DeviceIdType.MESH,
        )

    def part_copy(tap):
        return pltpu.make_async_remote_copy(
            src_ref=part_ref.at[tap], dst_ref=got_ref.at[tap],
            send_sem=part_send.at[tap], recv_sem=part_recv.at[tap],
            device_id={"rows": jnp.clip(me - distance * (tap - 1), 0, n - 1)},
            device_id_type=pl.DeviceIdType.MESH,
        )

    def inside(index):
        return jnp.logical_and(index >= 0, index < n)

    feat_copy.wait()

    @pl.loop(0, n)
    def _(k):
        cols = pl.ds(pl.multiple_of(k * part_chans, part_chans), part_chans)
        pre = feat_ref[:, cols].astype(F32) * scale_ref[:, cols] + shift_ref[:, cols]
        act = jnp.maximum(pre, 0.0).astype(BF16)
        act_ref[:, cols] = act
        send_ref[k] = act

    all_act[me] = send_ref[me]

    pl.semaphore_wait(barrier, n - 1)

    own_cot_copy.wait()

    @pl.when(mine + 1 < slow)
    def _():
        cot_copy(0, me).start()

    @pl.when(mine > 0)
    def _():
        cot_copy(1, me).start()

    cot_copy(2, me).start()
    cot_copy(3, me).start()

    def send_acts(first, count):
        @pl.loop(0, count)
        def _(t):
            act_copy(lax.rem(me + first + t, n), me).start()

    send_acts(1, 1)

    @pl.loop(0, 3)
    def _(q):
        tap = lax.rem(2 * q, 3)
        take_slow(q + 1)
        send_acts(2 + 1 * q, 1)
        w_copy(tap).wait()
        total = jnp.zeros((spots, outs), F32)
        for j in range(3):
            total = total + shifted(
                jnp.dot(act_ref[...], w_ref[tap, j], preferred_element_type=F32), j
            )
        part_ref[tap] = total.astype(BF16)

        @pl.when(tap == 1)
        def _():
            own_ref[...] = total

        @pl.when(jnp.logical_and(tap != 1, inside(me - distance * (tap - 1))))
        def _():
            part_copy(tap).start()

    @pl.loop(0, slow)
    def _(k):
        source = 4 * k + other_mid
        cot_copy(2, source).wait_recv()
        cot_copy(3, source).start()

    send_acts(5, 6)

    @pl.loop(0, slow)
    def _(k):
        cot_copy(3, 4 * k + other_core).wait_recv()
        cot_copy(3, 4 * k + lax.rem(other_core + 2, 4)).wait_recv()

    send_acts(11, 5)

    for i in range(3):
        source = me - distance * (i - 1)
        block = all_cot[jnp.clip(source, 0, n - 1)].astype(F32)
        block = jnp.where(inside(source), block, 0.0)
        for j in range(3):
            cot_sh[3 * i + j] = shifted(block, 2 - j).astype(BF16)

    step = 256

    @pl.loop(0, chans // step)
    def _(b):
        cols = pl.ds(pl.multiple_of(b * step, step), step)
        total = jnp.zeros((spots, step), F32)
        for i in range(3):
            for j in range(3):
                total = total + lax.dot_general(
                    cot_sh[3 * i + j], w_ref[i, j, cols, :],
                    (((1,), (1,)), ((), ())), preferred_element_type=F32,
                )
        scale = scale_ref[:, cols]
        pre = feat_ref[:, cols].astype(F32) * scale + shift_ref[:, cols]
        rounded = total.astype(BF16).astype(F32)
        fgrad_ref[:, cols] = (scale * jnp.where(pre > 0, rounded, 0.0)).astype(BF16)

    wgrad_ref[...] = jnp.zeros_like(wgrad_ref)

    @pl.loop(0, n)
    def _(k):
        source = lax.rem(me + n - k, n)

        @pl.when(k > 0)
        def _():
            act_copy(source, source).wait_recv()

        block = all_act[source].astype(F32)
        lhs = jnp.concatenate([shifted(block, j).astype(BF16) for j in range(3)], axis=1)
        for i in range(3):
            other = source - distance * (i - 1)

            @pl.when(inside(other))
            def _():
                wgrad_ref[i] += lax.dot_general(
                    lhs, all_cot[other], (((0,), (0,)), ((), ())),
                    preferred_element_type=F32,
                )

    for tap in (0, 2):

        @pl.when(inside(me + distance * (tap - 1)))
        def _():
            part_copy(tap).wait_recv()

        @pl.when(jnp.logical_not(inside(me + distance * (tap - 1))))
        def _():
            got_ref[tap] = jnp.zeros((spots, outs), BF16)

    branch_ref[...] = (own_ref[...] + got_ref[0].astype(F32) + got_ref[2].astype(F32)).astype(BF16)

    for tap in (0, 2):

        @pl.when(inside(me - distance * (tap - 1)))
        def _():
            part_copy(tap).wait_send()

    @pl.loop(1, n)
    def _(k):
        peer = lax.rem(me + k, n)
        act_copy(peer, me).wait_send()

    @pl.loop(0, slow)
    def _(k):
        source = 4 * k + low

        @pl.when(jnp.logical_and(k <= mine, mine + 1 < slow))
        def _():
            cot_copy(0, source).wait_send()

        @pl.when(jnp.logical_and(k >= mine, mine > 0))
        def _():
            cot_copy(1, source).wait_send()

        cot_copy(2, source).wait_send()
        cot_copy(3, source).wait_send()
        cot_copy(3, 4 * k + other_mid).wait_send()


def per_device_fused(features, bn_scale, bn_shift, atrous_weight, cotangent):
    rows, width, chans = features.shape
    outs = cotangent.shape[2]
    n = lax.axis_size("rows")
    spots = rows * width
    part = chans // n
    vmem = pl.BlockSpec(memory_space=pltpu.VMEM)
    anywhere = pl.BlockSpec(memory_space=pl.ANY)
    flops = 2 * 27 * spots * chans * outs
    dma = pltpu.SemaphoreType.DMA
    branch, fgrad, wgrad = pl.pallas_call(
        functools.partial(fused_kernel, n, rows, width, chans, outs),
        out_shape=(
            jax.ShapeDtypeStruct((spots, outs), BF16),
            jax.ShapeDtypeStruct((spots, chans), BF16),
            jax.ShapeDtypeStruct((3, 3 * part, outs), F32),
        ),
        in_specs=[anywhere, vmem, vmem, anywhere, anywhere],
        out_specs=(vmem, vmem, vmem),
        scratch_shapes=[
            pltpu.VMEM(atrous_weight.shape, BF16),
            pltpu.VMEM((spots, chans), BF16),
            pltpu.VMEM((spots, chans), BF16),
            pltpu.VMEM((n, spots, part), BF16),
            pltpu.VMEM((n, spots, part), BF16),
            pltpu.VMEM((n, spots, outs), BF16),
            pltpu.VMEM((9, spots, outs), BF16),
            pltpu.VMEM((spots, outs), F32),
            pltpu.VMEM((3, spots, outs), BF16),
            pltpu.VMEM((3, spots, outs), BF16),
            dma((3,)),
            dma((2,)),
            dma((n,)),
            dma((n,)),
            dma((4, n)),
            dma((n,)),
            dma((3,)),
            dma((3,)),
        ],
        compiler_params=pltpu.CompilerParams(
            collective_id=0, has_side_effects=True, vmem_limit_bytes=50 * 2**20
        ),
        cost_estimate=pl.CostEstimate(
            flops=flops, bytes_accessed=14 * 2**20, transcendentals=0
        ),
    )(
        features.reshape(spots, chans),
        bn_scale.reshape(1, chans),
        bn_shift.reshape(1, chans),
        atrous_weight,
        cotangent.reshape(spots, outs),
    )
    return (
        branch.reshape(rows, width, outs),
        fgrad.reshape(rows, width, chans),
        wgrad.reshape(3, 3, part, outs),
    )


def from_behind(array, axis, by):
    devices = lax.axis_size(axis)
    pairs = [(i, i + by) for i in range(devices) if 0 <= i + by < devices]
    return lax.ppermute(array, axis, pairs)


def branch_forward(blocks, atrous_weight, width):
    total = jnp.zeros(blocks[1].shape[:2] + (atrous_weight.shape[3],), jnp.float32)
    for row_tap in range(3):
        padded = jnp.pad(blocks[row_tap], ((0, 0), (RATE, RATE), (0, 0)))
        for col_tap in range(3):
            window = padded[:, RATE * col_tap : RATE * col_tap + width]
            total = total + jnp.einsum(
                "hwc,ck->hwk",
                window,
                atrous_weight[row_tap, col_tap],
                preferred_element_type=jnp.float32,
            )
    return total


def spatial_act_grad(blocks, atrous_weight, width):
    total = jnp.zeros(blocks[1].shape[:2] + (atrous_weight.shape[2],), jnp.float32)
    for row_tap in range(3):
        padded = jnp.pad(blocks[row_tap], ((0, 0), (RATE, RATE), (0, 0)))
        for col_tap in range(3):
            window = padded[:, RATE * (2 - col_tap) : RATE * (2 - col_tap) + width]
            total = total + jnp.einsum(
                "hwk,ck->hwc",
                window,
                atrous_weight[row_tap, col_tap],
                preferred_element_type=jnp.float32,
            )
    return total


def spatial_kernel_terms(blocks, cotangent, width):
    kernel_rows = []
    for row_tap in range(3):
        padded = jnp.pad(blocks[row_tap], ((0, 0), (RATE, RATE), (0, 0)))
        kernel_cols = []
        for col_tap in range(3):
            window = padded[:, RATE * col_tap : RATE * col_tap + width]
            kernel_cols.append(
                jnp.einsum("hwc,hwk->ck", window, cotangent, preferred_element_type=jnp.float32)
            )
        kernel_rows.append(jnp.stack(kernel_cols))
    return jnp.stack(kernel_rows)


def per_device_plain(features, bn_scale, bn_shift, atrous_weight, cotangent):
    local_rows, width, chans = features.shape
    distance = RATE // local_rows
    pre_act = features.astype(jnp.float32) * bn_scale + bn_shift
    activated = jnp.maximum(pre_act, 0.0).astype(jnp.bfloat16)
    act_above, cot_above = from_behind((activated, cotangent), "rows", distance)
    act_below, cot_below = from_behind((activated, cotangent), "rows", -distance)
    blocks = (act_above, activated, act_below)
    branch = branch_forward(blocks, atrous_weight, width)
    act_grad = spatial_act_grad((cot_below, cotangent, cot_above), atrous_weight, width)
    terms = spatial_kernel_terms(blocks, cotangent, width)
    weight_grad = lax.psum_scatter(terms, "rows", scatter_dimension=2, tiled=True)
    branch_out = branch.astype(jnp.bfloat16)
    rounded = lax.optimization_barrier(act_grad.astype(jnp.bfloat16)).astype(jnp.float32)
    feature_grad = (bn_scale * jnp.where(pre_act > 0, rounded, 0.0)).astype(jnp.bfloat16)
    return (branch_out, feature_grad, weight_grad)


def per_device(features, *others):
    rows, width, chans = features.shape
    fits = (
        lax.axis_size("rows") == 16
        and chans == 16 * LANES
        and RATE % rows == 0
        and width % 16 == 0
        and width > RATE
        and others[-1].shape[2] % LANES == 0
    )
    return (per_device_fused if fits else per_device_plain)(features, *others)


def solution(mesh):
    return jax.shard_map(
        per_device,
        mesh=mesh,
        in_specs=(
            P(("crops", "rows"), None, None),
            P(),
            P(),
            P(),
            P(("crops", "rows"), None, None),
        ),
        out_specs=(
            P(("crops", "rows"), None, None),
            P(("crops", "rows"), None, None),
            P("crops", None, "rows", None),
        ),
        check_vma=False,
    )
```
